1024 devices in a mesh: pipe: 16 (over x, y_hi), expert: 64 (over y_lo, z, core).
Axes of the slice: x: 8, y: 8 (y_hi: 2, y_lo: 4; y = y_hi * 4 + y_lo), z: 8, core: 2. Of those that a mesh axis runs over, the one named last changes fastest.
Arguments:
- hidden_a: bfloat16 [64, 768, 2048], P('expert'), may hold values from -6 to 6
- expert_weights: bfloat16 [64, 2048, 7168], P('expert', None, 'pipe'), may hold values from -0.125 to 0.125
- routes_a: int32 [4096, 8], P('expert'), may hold values from 0 to 63, all different within a row; in each aligned block of 64 rows (0 to 63, 64 to 127, ...) at most 12 rows name the same one
- gates_a: float32 [4096, 8], P('expert'), may hold values from 0.05 to 0.6
- cotangent_b: bfloat16 [4096, 7168], P('expert', 'pipe'), may hold values from -6 to 6
- routes_b: int32 [4096, 8], P('expert'), may hold values from 0 to 63, all different within a row; in each aligned block of 64 rows (0 to 63, 64 to 127, ...) at most 12 rows name the same one
- gates_b: float32 [4096, 8], P('expert'), may hold values from 0.05 to 0.6
Outputs:
- mixed_a: bfloat16 [4096, 7168], P('expert', 'pipe')
- grad_hidden_b: bfloat16 [64, 768, 2048], P('expert', None, 'pipe')
The draws below stay inside these ranges and needn't reach their ends.
Inputs may be any that keep to these rules, and one draw needn't show every extreme that they name: `routes_a`: among the tokens of one index of expert (aligned blocks of 64 rows), no expert is chosen more than 12 times, a bound that some block reaches; the 8 experts of a token differ. `routes_b`: among the tokens of one index of expert (aligned blocks of 64 rows), no expert is chosen more than 12 times, a bound that some block reaches; the 8 experts of a token differ.
All inputs are finite; a program needn't handle non-finite values.
Results may differ from the reference program's by a relative error of at most 0.019.
Values may be sent and summed in bfloat16 or wider, within the bound.
A program may use at most 64 MiB of HBM per device.

```python
import math
import jax
import jax.numpy as jnp
import numpy as np
from jax import lax

D = 7168
FF = 2048
TOP = 8
TOK_DEV = 64
EXPERTS = 64
CAP = 12
SLOTS = 768
TOKENS = 4096
N_PIPE = 16
N_EXPERT = 64


def levels(key, dims, pieces, least, largest):
    factor_of = 1.0
    for dim, parts in pieces:
        steps = jax.random.uniform(jax.random.fold_in(jax.random.fold_in(key, 6), dim), (parts,), jnp.float32, least / len(pieces), largest / len(pieces))
        factor_of = factor_of * jnp.repeat(jnp.exp(steps), dims[dim] // parts).reshape((-1,) + (1,) * (len(dims) - 1 - dim))
    return factor_of


def routed_block(key, own, number, rows, number_of, top, most, lean):
    sequence = jax.random.permutation(key, number_of)
    crowded, common = load_shares(number_of, rows * top, most, lean, True), load_shares(number_of, rows * top, most, lean, False)
    places = jnp.arange(number_of)

    def named(lengths, rotation):
        used = int((lengths > 0).sum())
        fixed = max(1, used // 4)
        moved = fixed + (places - fixed + rotation * (used - fixed)) % max(1, number_of - fixed)
        return jnp.zeros((number_of,), jnp.int32).at[sequence[jnp.where(places < fixed, places, moved)]].set(jnp.asarray(lengths, jnp.int32))

    lengths = jnp.where(number % 4 == 0, named(crowded, number // 4), named(common, number - number // 4 - 1))
    mixed = jax.random.permutation(jax.random.fold_in(own, 3), number_of)
    source_of, taker = mixed[0:number_of // 2 * 2:2], mixed[1:number_of // 2 * 2:2]
    margin = jnp.minimum(lengths[source_of] - 1, most - lengths[taker]) // 2
    margin = jnp.where((source_of == sequence[0]) | (taker == sequence[0]) | (lengths[taker] == 0), 0, jnp.maximum(margin, 0))
    moved = jax.random.randint(jax.random.fold_in(own, 4), (number_of // 2,), 0, 1 << 20) % (margin + 1)
    lengths = lengths.at[source_of].add(-moved).at[taker].add(moved)
    members = jnp.searchsorted(jnp.cumsum(lengths), jnp.arange(rows * top), side="right").astype(jnp.int32)
    listing = members.reshape(top, rows).T
    listing = listing[jax.random.permutation(jax.random.fold_in(own, 1), rows)]
    rotation = jax.random.randint(jax.random.fold_in(own, 2), (rows, 1), 0, top)
    return jnp.take_along_axis(listing, (jnp.arange(top)[None, :] + rotation) % top, axis=1)


def load_shares(number_of, total, limit, lean, full):
    portions = [(1 << 20) // math.isqrt(standing ** lean) + 1 for standing in range(1, number_of + 1)]
    largest = limit if full else min(limit, max(-(-total // number_of), total * portions[0] // sum(portions)))
    least = 1 if total - largest >= number_of - 1 else 0
    holding, surplus = [largest] + [least] * (number_of - 1), total - largest - least * (number_of - 1)
    while surplus > 0:
        candidates = [i for i in range(1, number_of) if holding[i] < largest] or [i for i in range(1, number_of) if holding[i] < limit]
        mass, budget = sum([portions[i] for i in candidates]), surplus
        for i in candidates:
            extra = min(limit - holding[i], max(1, budget * portions[i] // mass), surplus)
            holding[i] = holding[i] + extra
            surplus = surplus - extra
    return np.array(holding)


def noise(own_key, extent, width, bound, split=(), kind=jnp.bfloat16):
    values = width * jax.random.normal(own_key, extent, jnp.float32)
    if split:
        values = values * levels(own_key, extent, split, -0.22, 0.18)
    return jnp.clip(values, -bound, bound).astype(kind)


def setup_inputs(seed: int = 0) -> dict:
    keys = jax.random.split(jax.random.key(seed), 8)
    hidden_a = noise(keys[0], (EXPERTS, SLOTS, FF), 1.0, 6.0, ((0, 64),))
    expert_weights = noise(keys[1], (EXPERTS, FF, D), FF ** -0.5, 0.125, ((0, 64), (2, 16)))
    routes_a_keys = jax.random.split(jax.random.fold_in(keys[2], 1), TOKENS // TOK_DEV)
    routes_a_turns = jax.random.permutation(jax.random.fold_in(keys[2], 3), TOKENS // TOK_DEV)
    routes_a = jax.vmap(lambda own, number: routed_block(jax.random.fold_in(keys[2], 2), own, number, TOK_DEV, EXPERTS, TOP, CAP, 2))(routes_a_keys, routes_a_turns).reshape((TOKENS, TOP))
    gates_a = jnp.clip(jnp.exp(math.log(0.6) - 2.4849067 * jax.random.uniform(keys[3], (TOKENS, TOP), jnp.float32) ** levels(keys[3], (TOKENS, TOP), ((0, 64),), -0.2, 0.2)), 0.05, 0.6)
    cotangent_b = noise(keys[4], (TOKENS, D), 1.0, 6.0, ((0, 64), (1, 16)))
    routes_b_keys = jax.random.split(jax.random.fold_in(keys[5], 1), TOKENS // TOK_DEV)
    routes_b_turns = jax.random.permutation(jax.random.fold_in(keys[5], 3), TOKENS // TOK_DEV)
    routes_b = jax.vmap(lambda own, number: routed_block(jax.random.fold_in(keys[5], 2), own, number, TOK_DEV, EXPERTS, TOP, CAP, 2))(routes_b_keys, routes_b_turns).reshape((TOKENS, TOP))
    gates_b = jnp.clip(jnp.exp(math.log(0.6) - 2.4849067 * jax.random.uniform(keys[6], (TOKENS, TOP), jnp.float32) ** levels(keys[6], (TOKENS, TOP), ((0, 64),), -0.2, 0.2)), 0.05, 0.6)
    return dict(hidden_a=hidden_a, expert_weights=expert_weights, routes_a=routes_a, gates_a=gates_a, cotangent_b=cotangent_b, routes_b=routes_b, gates_b=gates_b)


def slot_rows(routes):
    blocks = routes.reshape(N_EXPERT, TOK_DEV * TOP)
    onehot = (blocks[:, :, None] == jnp.arange(EXPERTS, dtype=jnp.int32)[None, None, :]).astype(jnp.int32)
    ranks = jnp.cumsum(onehot, axis=1) - onehot
    slots = jnp.sum(ranks * onehot, axis=2).reshape(N_EXPERT * TOK_DEV, TOP)
    source = (jnp.arange(N_EXPERT * TOK_DEV, dtype=jnp.int32) // TOK_DEV)[:, None]
    return routes * (N_EXPERT * CAP) + source * CAP + slots


def reference(hidden_a, expert_weights, routes_a, gates_a, cotangent_b, routes_b, gates_b):
    def forward_one(pair):
        return jnp.dot(pair[0], pair[1], preferred_element_type=jnp.float32).astype(jnp.bfloat16)

    expert_out = lax.map(forward_one, (hidden_a, expert_weights))
    index_a = slot_rows(routes_a)
    picked = expert_out.reshape(-1, D)[index_a]
    mixed_a = jnp.einsum('tk,tkd->td', gates_a.astype(jnp.float32), picked.astype(jnp.float32)).astype(jnp.bfloat16)
    index_b = slot_rows(routes_b)
    values = (gates_b[:, :, None] * cotangent_b[:, None, :].astype(jnp.float32)).astype(jnp.bfloat16)
    slot_grad = jnp.zeros((EXPERTS * N_EXPERT * CAP, D), jnp.bfloat16)
    slot_grad = slot_grad.at[index_b.reshape(-1)].set(values.reshape(-1, D))
    slot_grad = slot_grad.reshape(EXPERTS, N_EXPERT * CAP, D)

    def backward_one(pair):
        blocks_g = pair[0].reshape(N_EXPERT * CAP, N_PIPE, D // N_PIPE).astype(jnp.float32)
        blocks_w = pair[1].reshape(FF, N_PIPE, D // N_PIPE).astype(jnp.float32)
        partial_value = jnp.einsum('rpd,fpd->prf', blocks_g, blocks_w).astype(jnp.bfloat16)
        partial_value = lax.optimization_barrier(partial_value)
        return jnp.sum(partial_value.astype(jnp.float32), axis=0).astype(jnp.bfloat16)

    grad_hidden_b = lax.map(backward_one, (slot_grad, expert_weights))
    return mixed_a, grad_hidden_b
```

```python
import functools

import jax
import jax.numpy as jnp
from jax import lax
from jax.experimental import pallas as pl
from jax.experimental.pallas import tpu as pltpu
from jax.sharding import PartitionSpec as P

NX, NYH = 8, 2
NY, NZ, NC = 4, 8, 2
SEND_A, COMBINE_A = 1, 9

BF16, F32 = jnp.bfloat16, jnp.float32


def body(
    cap,
    h_hbm, w_hbm, ra_ref, ga_ref, cot_ref, rb_ref, gb_ref,
    mixed_ref, grad_ref,
    h_vm, w_vm, gath, codes, fwd, tile48, asend, arecv, bsend, brecv, pa,
    pbuf, splus, sminus, rplus, rminus, fin, hsend, hrecv, out4, gout,
    dense, dsend, drecv,
    load_sem, y_s, y_r, az_s, az_r, bz_s, bz_r, xp_s, xp_r, xm_s, xm_r,
    h_s, h_r, d_s, d_r,
):
    tok, width = cot_ref.shape
    top = ra_ref.shape[1]
    total = NY * NZ * NC
    msg = NY * cap
    half = NX // 2
    wide = gath.shape[2]
    p = lax.axis_index("pipe")
    e = lax.axis_index("expert")
    x, yh = p // NYH, p % NYH
    y, z, c = e // (NZ * NC), (e // NC) % NZ, e % NC

    def dev(x=x, yh=yh, y=y, z=z, c=c):
        return {"pipe": x * NYH + yh, "expert": (y * NZ + z) * NC + c}

    def z_step(k):
        if isinstance(k, int):
            return (k + 1) // 2 if k % 2 else (NZ - k // 2) % NZ
        return lax.select(k % 2 == 1, (k + 1) // 2, (NZ - k // 2) % NZ)

    def remote(src, dst, send, recv, to):
        return pltpu.make_async_remote_copy(
            src_ref=src, dst_ref=dst, send_sem=send, recv_sem=recv,
            device_id=to, device_id_type=pl.DeviceIdType.MESH,
        )

    load_w = pltpu.make_async_copy(w_hbm, w_vm, load_sem.at[0])
    load_h = pltpu.make_async_copy(h_hbm, h_vm, load_sem.at[1])
    load_w.start()
    load_h.start()

    partners = [dev(y=(y + d) % NY) for d in range(1, NY)]
    partners += [
        dev(z=(z + d) % NZ, c=(c + f) % NC)
        for d in range(NZ) for f in range(NC) if d or f
    ]
    partners += [dev(x=(x + 1) % NX), dev(x=(x + NX - 1) % NX), dev(yh=1 - yh)]
    barrier = pltpu.get_barrier_semaphore()
    for to in partners:
        pl.semaphore_signal(
            barrier, inc=1, device_id=to, device_id_type=pl.DeviceIdType.MESH
        )

    lane = lax.broadcasted_iota(jnp.int32, (tok, 128), 1)
    base = width - (wide - 128)
    tail = jnp.dot(
        cot_ref[:, wide - 128:],
        (
            lax.broadcasted_iota(jnp.int32, (base, 128), 0)
            == lax.broadcasted_iota(jnp.int32, (base, 128), 1)
        ).astype(F32).astype(BF16),
        preferred_element_type=F32,
    )
    before = (
        lax.broadcasted_iota(jnp.int32, (tok, tok), 0)
        > lax.broadcasted_iota(jnp.int32, (tok, tok), 1)
    ).astype(F32).astype(BF16)
    for n, (r_ref, g_ref) in enumerate(((ra_ref, ga_ref), (rb_ref, gb_ref))):
        first = base + n * 4 * 8
        routes = r_ref[...]
        gates = g_ref[...]
        high = gates.astype(BF16).astype(F32)
        low = (gates - high).astype(BF16).astype(F32)
        names = routes.astype(F32)
        hit = [routes[:, k:k + 1] == lane for k in range(top)]
        member = jnp.zeros((tok, 128), F32)
        for k in range(top):
            member = jnp.where(hit[k], 1.0, member)
        rank = jnp.dot(before, member.astype(BF16), preferred_element_type=F32)
        for k in range(top):
            slot = jnp.sum(jnp.where(hit[k], rank, 0.0), axis=1, keepdims=True)
            tail = jnp.where(lane == first + k, names[:, k:k + 1], tail)
            tail = jnp.where(lane == first + 8 + k, slot, tail)
            tail = jnp.where(lane == first + 16 + k, high[:, k:k + 1], tail)
            tail = jnp.where(lane == first + 24 + k, low[:, k:k + 1], tail)
    gath[0, :, :wide - 128] = cot_ref[:, :wide - 128]
    gath[0, :, wide - 128:] = tail.astype(BF16)

    pl.semaphore_wait(barrier, len(partners))

    def y_copy(d):
        return remote(
            gath.at[0], gath.at[d], y_s.at[d - 1], y_r.at[d - 1],
            dev(y=(y + d) % NY),
        )

    for d in (2, 1, 3):
        if d < NY:
            y_copy(d).start()

    load_w.wait()
    load_h.wait()
    rows = NZ * NC * cap

    def forward(j, carry):
        value = jnp.dot(
            h_vm[pl.ds(pl.multiple_of(j * rows, 16), rows), :], w_vm[...],
            preferred_element_type=F32,
        )
        for i in range(NZ * NC):
            fwd[j * (NZ * NC) + i, 0:cap, :] = value[i * cap:(i + 1) * cap, :]
        return carry

    lax.fori_loop(0, NY, forward, 0)

    def pack_a(k, carry):
        to = ((z + z_step(k)) % NZ) * NC
        for f in range(NC):
            for r in range(NY):
                source = ((y + NY - r) % NY) * (NZ * NC) + to + (c + f) % NC
                tile48[r * cap:(r + 1) * cap, :] = fwd[source, 0:cap, :]
            asend[k * NC + f] = tile48[...].astype(BF16)
        return carry

    lax.fori_loop(0, NZ, pack_a, 0)
    arecv[0] = asend[0]

    for d in range(1, NY):
        y_copy(d).wait_recv()

    for n in range(2):
        for r in range(NY):
            info = gath[r, :, wide - 128:].astype(F32).T
            first = base + n * 4 * 8
            cols = slice(r * tok, (r + 1) * tok)
            codes[n, 0, :, cols] = (
                info[first:first + 8] * 16.0 + info[first + 8:first + 16]
            )
            codes[n, 1, :, cols] = info[first + 16:first + 24]
            codes[n, 2, :, cols] = info[first + 24:first + 32]

    row = lax.broadcasted_iota(jnp.int32, (msg, NY * tok), 0)
    col = lax.broadcasted_iota(jnp.int32, (msg, NY * tok), 1)
    slot_code = jnp.full((msg, NY * tok), -4096.0, F32)
    for r in range(NY):
        inside = (
            (row >= r * cap) & (row < (r + 1) * cap)
            & (col >= r * tok) & (col < (r + 1) * tok)
        )
        slot_code = jnp.where(inside, (row - r * cap).astype(F32), slot_code)

    def pairs(n, expert):
        want = slot_code + (expert * 16).astype(F32)
        high = jnp.zeros((msg, NY * tok), F32)
        low = jnp.zeros((msg, NY * tok), F32)
        for k in range(top):
            same = want == codes[n, 0, k:k + 1, :]
            high = jnp.where(same, codes[n, 1, k:k + 1, :], high)
            low = jnp.where(same, codes[n, 2, k:k + 1, :], low)
        return high.astype(BF16), low.astype(BF16)

    def bz_copy(k, f):
        m = k * NC + f
        return remote(
            bsend.at[m], brecv.at[m], bz_s.at[m], bz_r.at[m],
            dev(z=(z + z_step(k)) % NZ, c=(c + f) % NC),
        )

    def az_copy(k, f):
        m = k * NC + f
        return remote(
            asend.at[m], arecv.at[m], az_s.at[m], az_r.at[m],
            dev(z=(z + z_step(k)) % NZ, c=(c + f) % NC),
        )

    def fill(k, f):
        expert = (y * NZ + (z + z_step(k)) % NZ) * NC + (c + f) % NC
        high, low = pairs(1, expert)
        cots = gath[...].reshape(NY * tok, wide)
        value = jnp.dot(high, cots, preferred_element_type=F32)
        value += jnp.dot(low, cots, preferred_element_type=F32)
        return value[:, :width].astype(BF16)

    for f in range(1, NC):
        bsend[f] = fill(0, f)
        bz_copy(0, f).start()

    def fill_step(k, carry):
        for f in range(NC):
            bsend[k * NC + f] = fill(k, f)
            bz_copy(k, f).start()
        return carry

    lax.fori_loop(1, NZ, fill_step, 0)
    brecv[0] = fill(0, 0)

    block = NC * msg

    def plus(k, s):
        to, sems = dev(x=(x + 1) % NX), (xp_s.at[k, s], xp_r.at[k, s])
        if s == 0:
            return remote(splus.at[k, s, 0], rplus.at[k, s, 0], *sems, to)
        return remote(splus.at[k, s], rplus.at[k, s], *sems, to)

    def minus(k, s):
        to, sems = dev(x=(x + NX - 1) % NX), (xm_s.at[k, s], xm_r.at[k, s])
        if s == 0:
            return remote(sminus.at[k, s, 1], rminus.at[k, s, 1], *sems, to)
        return remote(sminus.at[k, s], rminus.at[k, s], *sems, to)

    def swap(k):
        return remote(
            hsend.at[k], hrecv.at[k], h_s.at[k], h_r.at[k], dev(yh=1 - yh)
        )

    def product(k):
        @pl.when(k > 0)
        def _():
            bz_copy(k, 0).wait_recv()

        for f in range(1, NC):
            bz_copy(k, f).wait_recv()
        value = brecv[pl.ds(k * NC, NC)].reshape(block, width)
        order = [half]
        for i in range(half - 1, 0, -1):
            order += [i, NX - i]
        for off in order + [0]:
            q = (x + off) % NX
            part = lax.dot_general(
                value, w_vm[pl.ds(pl.multiple_of(q * 256, 256), 256), :],
                (((1,), (1,)), ((), ())), preferred_element_type=F32,
            )
            if off == half:
                splus[k, 0, 0] = part[:, :128].astype(BF16)
                plus(k, 0).start()
                sminus[k, 0, 1] = part[:, 128:].astype(BF16)
                minus(k, 0).start()
            else:
                pbuf[k, off, 0] = part[:, :128]
                pbuf[k, off, 1] = part[:, 128:]

    def pass_on(k, s):
        plus(k, s - 1).wait_recv()
        for h in range(2):
            value = pbuf[k, half - s, h]
            if s > 1 or h == 0:
                value += rplus[k, s - 1, h].astype(F32)
            splus[k, s, h] = value.astype(BF16)
        plus(k, s).start()
        minus(k, s - 1).wait_recv()
        for h in range(2):
            value = pbuf[k, half + s, h]
            if s > 1 or h == 1:
                value += rminus[k, s - 1, h].astype(F32)
            sminus[k, s, h] = value.astype(BF16)
        minus(k, s).start()

    def collect(k):
        plus(k, half - 1).wait_recv()
        minus(k, half - 1).wait_recv()
        for h in range(2):
            value = pbuf[k, 0, h] + rplus[k, half - 1, h].astype(F32)
            fin[k, h] = value + rminus[k, half - 1, h].astype(F32)
        hsend[k] = fin[k, 1 - yh].astype(BF16)
        swap(k).start()

    def finish(k):
        swap(k).wait_recv()
        fin[k, 0] = fin[k, yh] + hrecv[k].astype(F32)
        at = ((z + NZ - z_step(k)) % NZ) * NC
        for f in range(NC):
            for r in range(NY):
                source = ((y + NY - r) % NY) * (NZ * NC) + at + (c + f) % NC
                start = f * msg + r * cap
                out4[source, 0:cap, :] = fin[k, 0, start:start + cap, :]

    def d_copy(r):
        return remote(
            dsend.at[r - 1], drecv.at[r - 1], d_s.at[r - 1], d_r.at[r - 1],
            dev(y=(y + NY - r) % NY),
        )

    def combine():
        def one(k, carry):
            for f in range(NC):
                m = k * NC + f
                expert = (y * NZ + (z + NZ - z_step(k)) % NZ) * NC + (c + f) % NC
                high, low = pairs(0, expert)
                at = pl.ds(pl.multiple_of(m * msg, 16), msg)
                pa[0, at, :] = high
                pa[1, at, :] = low
            return carry

        lax.fori_loop(0, NZ, one, 0)
        for m in range(1, NZ * NC):
            az_copy(m // NC, m % NC).wait_recv()
        arrived = arecv[...].reshape(total * cap, width)
        over_rows = (((0,), (0,)), ((), ()))
        value = lax.dot_general(
            pa[0], arrived, over_rows, preferred_element_type=F32
        )
        value += lax.dot_general(
            pa[1], arrived, over_rows, preferred_element_type=F32
        )
        for r in range(1, NY):
            dsend[r - 1] = value[r * tok:(r + 1) * tok].astype(BF16)
            d_copy(r).start()
        dense[...] = value[:tok]

    def step(t, carry):
        def at(s, run):
            @pl.when((t >= s) & (t < s + NZ))
            def _():
                run(t - s)

        at(half + 1, finish)
        at(half, collect)
        for s in range(half - 1, 0, -1):
            at(s, functools.partial(pass_on, s=s))
        at(0, product)

        @pl.when(t == SEND_A)
        def _():
            for m in range(1, NZ * NC):
                az_copy(m // NC, m % NC).start()

        @pl.when(t == COMBINE_A)
        def _():
            combine()

        return carry

    lax.fori_loop(0, NZ + half + 2, step, 0)

    for i in range(total):
        gout[i * cap:(i + 1) * cap, :] = out4[i, 0:cap, :]
    grad_ref[...] = gout[...].astype(BF16)

    result = dense[...]
    for r in range(1, NY):
        d_copy(r).wait_recv()
        result += drecv[r - 1].astype(F32)
    mixed_ref[...] = result.astype(BF16)

    for d in range(1, NY):
        y_copy(d).wait_send()
        d_copy(d).wait_send()

    def sent_z(m, carry):
        for f in range(NC):
            if f == 0:
                @pl.when(m > 0)
                def _():
                    bz_copy(m, 0).wait_send()
                    az_copy(m, 0).wait_send()
            else:
                bz_copy(m, f).wait_send()
                az_copy(m, f).wait_send()
        for s in range(half):
            plus(m, s).wait_send()
            minus(m, s).wait_send()
        swap(m).wait_send()
        return carry

    lax.fori_loop(0, NZ, sent_z, 0)


def on_device(hidden_a, expert_weights, routes_a, gates_a, cotangent_b, routes_b, gates_b):
    total = NY * NZ * NC
    _, slots, ff = hidden_a.shape
    cap = slots // total
    tok, width = cotangent_b.shape
    wide = -(-width // 128) * 128
    half, msg, block = NX // 2, NY * cap, NY * cap * NC
    count = NZ * NC
    vm, dma = pltpu.VMEM, pltpu.SemaphoreType.DMA
    whole = pl.BlockSpec(memory_space=pltpu.VMEM)
    anywhere = pl.BlockSpec(memory_space=pl.ANY)
    mixed, grad = pl.pallas_call(
        functools.partial(body, cap),
        out_shape=(
            jax.ShapeDtypeStruct((tok, width), BF16),
            jax.ShapeDtypeStruct((slots, 128), BF16),
        ),
        in_specs=[anywhere, anywhere] + [whole] * 5,
        out_specs=(whole, whole),
        scratch_shapes=[
            vm((slots, ff), BF16),
            vm((ff, width), BF16),
            vm((NY, tok, wide), BF16),
            vm((2, 3, 8, NY * tok), F32),
            vm((total, 16, width), F32),
            vm((msg, width), F32),
            vm((count, msg, width), BF16),
            vm((count, msg, width), BF16),
            vm((count, msg, width), BF16),
            vm((count, msg, width), BF16),
            vm((2, slots, NY * tok), BF16),
            vm((NZ, NX, 2, block, 128), F32),
            vm((NZ, half, 2, block, 128), BF16),
            vm((NZ, half, 2, block, 128), BF16),
            vm((NZ, half, 2, block, 128), BF16),
            vm((NZ, half, 2, block, 128), BF16),
            vm((NZ, 2, block, 128), F32),
            vm((NZ, block, 128), BF16),
            vm((NZ, block, 128), BF16),
            vm((total, 16, 128), F32),
            vm((slots, 128), F32),
            vm((tok, width), F32),
            vm((NY - 1, tok, width), BF16),
            vm((NY - 1, tok, width), BF16),
            dma((2,)),
            dma((NY - 1,)), dma((NY - 1,)),
            dma((count,)), dma((count,)),
            dma((count,)), dma((count,)),
            dma((NZ, half)), dma((NZ, half)),
            dma((NZ, half)), dma((NZ, half)),
            dma((NZ,)), dma((NZ,)),
            dma((NY - 1,)), dma((NY - 1,)),
        ],
        compiler_params=pltpu.CompilerParams(
            collective_id=0, has_side_effects=True,
            vmem_limit_bytes=56 * 1024 * 1024,
        ),
    )(
        hidden_a.reshape(slots, ff), expert_weights.reshape(ff, width),
        routes_a, gates_a, cotangent_b, routes_b, gates_b,
    )
    return mixed, grad.reshape(1, slots, 128)


def solution(mesh):
    in_specs = (
        P("expert", None, None),
        P("expert", None, "pipe"),
        P("expert", None),
        P("expert", None),
        P("expert", "pipe"),
        P("expert", None),
        P("expert", None),
    )
    out_specs = (P("expert", "pipe"), P("expert", None, "pipe"))
    return jax.shard_map(
        on_device, mesh=mesh, in_specs=in_specs, out_specs=out_specs, check_vma=False
    )
```

```python
import functools

import jax
import jax.numpy as jnp
from jax import lax
from jax.experimental import pallas as pl
from jax.experimental.pallas import tpu as pltpu
from jax.sharding import PartitionSpec as P

NX, NYH = 8, 2
NY, NZ, NC = 4, 8, 2
SEND_A, COMBINE_A = 4, 13
LAG, SWAP_LAG = 2, 3

BF16, F32 = jnp.bfloat16, jnp.float32


def body(
    cap,
    h_hbm, w_hbm, ra_ref, ga_ref, cot_ref, rb_ref, gb_ref,
    mixed_ref, grad_ref,
    h_vm, w_vm, gath, codes, fwd, tile48, asend, arecv, bsend, brecv, pa,
    pbuf, splus, sminus, rplus, rminus, fin, hsend, hrecv, out4, gout,
    dense, dsend, drecv,
    load_sem, y_s, y_r, az_s, az_r, bz_s, bz_r, xp_s, xp_r, xm_s, xm_r,
    h_s, h_r, d_s, d_r,
):
    tok, width = cot_ref.shape
    top = ra_ref.shape[0]
    total = NY * NZ * NC
    msg = NY * cap
    half = NX // 2
    wide = gath.shape[2]
    p = lax.axis_index("pipe")
    e = lax.axis_index("expert")
    x, yh = p // NYH, p % NYH
    y, z, c = e // (NZ * NC), (e // NC) % NZ, e % NC

    def dev(x=x, yh=yh, y=y, z=z, c=c):
        return {"pipe": x * NYH + yh, "expert": (y * NZ + z) * NC + c}

    def z_step(k):
        if isinstance(k, int):
            return (k + 1) // 2 if k % 2 else (NZ - k // 2) % NZ
        return lax.select(k % 2 == 1, (k + 1) // 2, (NZ - k // 2) % NZ)

    def remote(src, dst, send, recv, to):
        return pltpu.make_async_remote_copy(
            src_ref=src, dst_ref=dst, send_sem=send, recv_sem=recv,
            device_id=to, device_id_type=pl.DeviceIdType.MESH,
        )

    load_w = pltpu.make_async_copy(w_hbm, w_vm, load_sem.at[0])
    load_h = pltpu.make_async_copy(h_hbm, h_vm, load_sem.at[1])
    load_w.start()
    load_h.start()

    partners = [dev(y=(y + d) % NY) for d in range(1, NY)]
    partners += [
        dev(z=(z + d) % NZ, c=(c + f) % NC)
        for d in range(NZ) for f in range(NC) if d or f
    ]
    partners += [dev(x=(x + 1) % NX), dev(x=(x + NX - 1) % NX), dev(yh=1 - yh)]
    barrier = pltpu.get_barrier_semaphore()
    for to in partners:
        pl.semaphore_signal(
            barrier, inc=1, device_id=to, device_id_type=pl.DeviceIdType.MESH
        )

    base = width - (wide - 128)

    def mask(test, shape):
        rows = lax.broadcasted_iota(jnp.int32, shape, 0)
        cols = lax.broadcasted_iota(jnp.int32, shape, 1)
        return test(rows, cols).astype(F32).astype(BF16)

    after = mask(lambda i, j: i < j, (tok, tok))
    expert_row = lax.broadcasted_iota(jnp.int32, (total, tok), 0)
    notes = []
    for r_ref, g_ref in ((ra_ref, ga_ref), (rb_ref, gb_ref)):
        routes = r_ref[...]
        gates = g_ref[...]
        high = gates.astype(BF16)
        low = (gates - high.astype(F32)).astype(BF16)
        hit = [routes[k:k + 1, :] == expert_row for k in range(top)]
        member = jnp.zeros((total, tok), F32)
        for k in range(top):
            member = jnp.where(hit[k], 1.0, member)
        rank = jnp.dot(member.astype(BF16), after, preferred_element_type=F32)
        slot = [
            jnp.sum(jnp.where(hit[k], rank, 0.0), axis=0, keepdims=True)
            for k in range(top)
        ]
        notes += [routes.astype(F32), jnp.concatenate(slot, axis=0)]
        notes += [high.astype(F32), low.astype(F32)]
    tail = jnp.dot(
        cot_ref[:, wide - 128:], mask(lambda i, j: i == j, (base, 128)),
        preferred_element_type=F32,
    )
    tail += jnp.dot(
        jnp.concatenate(notes, axis=0).astype(BF16),
        mask(lambda i, j: i + base == j, (tok, 128)),
        preferred_element_type=F32,
    )
    gath[0, :, :wide - 128] = cot_ref[:, :wide - 128]
    gath[0, :, wide - 128:] = tail.astype(BF16)

    pl.semaphore_wait(barrier, len(partners))

    def y_copy(d):
        return remote(
            gath.at[0], gath.at[d], y_s.at[d - 1], y_r.at[d - 1],
            dev(y=(y + d) % NY),
        )

    for d in (2, 1, 3):
        if d < NY:
            y_copy(d).start()

    load_w.wait()
    load_h.wait()
    rows = NZ * NC * cap

    def forward(j, carry):
        value = lax.dot_general(
            h_vm[pl.ds(pl.multiple_of(j * rows, 16), rows), :], w_vm[...],
            (((1,), (1,)), ((), ())), preferred_element_type=F32,
        )
        for i in range(NZ * NC):
            fwd[j * (NZ * NC) + i, 0:cap, :] = value[i * cap:(i + 1) * cap, :]
        return carry

    lax.fori_loop(0, NY, forward, 0)

    def pack_a(k, carry):
        to = ((z + z_step(k)) % NZ) * NC
        for f in range(NC):
            for r in range(NY):
                source = ((y + NY - r) % NY) * (NZ * NC) + to + (c + f) % NC
                tile48[r * cap:(r + 1) * cap, :] = fwd[source, 0:cap, :]
            asend[k * NC + f] = tile48[...].astype(BF16)
        return carry

    lax.fori_loop(0, NZ, pack_a, 0)
    arecv[0] = asend[0]

    for d in range(1, NY):
        y_copy(d).wait_recv()

    for r in range(0, NY, 2):
        left = pltpu.roll(gath[r, :, wide - 128:].astype(F32), 128 - base, 1)
        right = gath[r + 1, :, wide - 128:].astype(F32)
        lane = lax.broadcasted_iota(jnp.int32, (tok, 128), 1)
        info = jnp.where(lane < tok, left, right)
        cols = slice(r * tok, (r + 2) * tok)
        for n in range(2):
            at = n * 4 * 8
            codes[n, 0, :, cols] = info[at:at + 8] * 16.0 + info[at + 8:at + 16]
            codes[n, 1, :, cols] = info[at + 16:at + 24]
            codes[n, 2, :, cols] = info[at + 24:at + 32]

    row = lax.broadcasted_iota(jnp.int32, (msg, NY * tok), 0)
    col = lax.broadcasted_iota(jnp.int32, (msg, NY * tok), 1)
    slot_code = jnp.full((msg, NY * tok), -4096.0, F32)
    for r in range(NY):
        inside = (
            (row >= r * cap) & (row < (r + 1) * cap)
            & (col >= r * tok) & (col < (r + 1) * tok)
        )
        slot_code = jnp.where(inside, (row - r * cap).astype(F32), slot_code)

    def pairs(n, expert):
        want = slot_code + (expert * 16).astype(F32)
        high = jnp.zeros((msg, NY * tok), F32)
        low = jnp.zeros((msg, NY * tok), F32)
        for k in range(top):
            same = want == codes[n, 0, k:k + 1, :]
            high = jnp.where(same, codes[n, 1, k:k + 1, :], high)
            low = jnp.where(same, codes[n, 2, k:k + 1, :], low)
        return high.astype(BF16), low.astype(BF16)

    def bz_copy(k, f):
        m = k * NC + f
        return remote(
            bsend.at[m], brecv.at[m], bz_s.at[m], bz_r.at[m],
            dev(z=(z + z_step(k)) % NZ, c=(c + f) % NC),
        )

    def az_copy(k, f):
        m = k * NC + f
        return remote(
            asend.at[m], arecv.at[m], az_s.at[m], az_r.at[m],
            dev(z=(z + z_step(k)) % NZ, c=(c + f) % NC),
        )

    def fill(k, f):
        expert = (y * NZ + (z + z_step(k)) % NZ) * NC + (c + f) % NC
        high, low = pairs(1, expert)
        cots = gath[...].reshape(NY * tok, wide)
        value = jnp.dot(
            jnp.concatenate([high, low], axis=0), cots, preferred_element_type=F32
        )
        return (value[:msg, :width] + value[msg:, :width]).astype(BF16)

    for f in range(1, NC):
        bsend[f] = fill(0, f)
        bz_copy(0, f).start()
    brecv[0] = fill(0, 0)

    def fill_step(k, carry):
        for f in range(NC):
            bsend[k * NC + f] = fill(k, f)
            bz_copy(k, f).start()
        return carry

    block = NC * msg
    blocks = NZ

    def plus(k, s):
        to, sems = dev(x=(x + 1) % NX), (xp_s.at[k, s], xp_r.at[k, s])
        if s == 0:
            return remote(splus.at[k, s, 0], rplus.at[k, s, 0], *sems, to)
        return remote(splus.at[k, s], rplus.at[k, s], *sems, to)

    def minus(k, s):
        to, sems = dev(x=(x + NX - 1) % NX), (xm_s.at[k, s], xm_r.at[k, s])
        if s == 0:
            return remote(sminus.at[k, s, 1], rminus.at[k, s, 1], *sems, to)
        return remote(sminus.at[k, s], rminus.at[k, s], *sems, to)

    def swap(k):
        return remote(
            hsend.at[k], hrecv.at[k], h_s.at[k], h_r.at[k], dev(yh=1 - yh)
        )

    def product(k):
        if isinstance(k, int):
            for f in range(1, NC):
                bz_copy(k, f).wait_recv()
        else:
            for f in range(NC):
                bz_copy(k, f).wait_recv()
        value = brecv[pl.ds(k * NC, NC)].reshape(block, width)
        order = [half]
        for i in range(half - 1, 0, -1):
            order += [i, NX - i]
        for off in order + [0]:
            q = (x + off) % NX
            part = jnp.dot(
                value, w_vm[:, pl.ds(pl.multiple_of(q * 256, 256), 256)],
                preferred_element_type=F32,
            )
            if off == half:
                splus[k, 0, 0] = part[:, :128].astype(BF16)
                plus(k, 0).start()
                sminus[k, 0, 1] = part[:, 128:].astype(BF16)
                minus(k, 0).start()
            else:
                pbuf[k, off, 0] = part[:, :128]
                pbuf[k, off, 1] = part[:, 128:]

    def pass_on(k, s):
        plus(k, s - 1).wait_recv()
        for h in range(2):
            value = pbuf[k, half - s, h]
            if s > 1 or h == 0:
                value += rplus[k, s - 1, h].astype(F32)
            splus[k, s, h] = value.astype(BF16)
        plus(k, s).start()
        minus(k, s - 1).wait_recv()
        for h in range(2):
            value = pbuf[k, half + s, h]
            if s > 1 or h == 1:
                value += rminus[k, s - 1, h].astype(F32)
            sminus[k, s, h] = value.astype(BF16)
        minus(k, s).start()

    def collect(k):
        plus(k, half - 1).wait_recv()
        minus(k, half - 1).wait_recv()
        for h in range(2):
            value = pbuf[k, 0, h] + rplus[k, half - 1, h].astype(F32)
            fin[k, h] = value + rminus[k, half - 1, h].astype(F32)
        hsend[k] = fin[k, 1 - yh].astype(BF16)
        swap(k).start()

    def finish(k):
        swap(k).wait_recv()
        fin[k, 0] = fin[k, yh] + hrecv[k].astype(F32)
        at = ((z + NZ - z_step(k)) % NZ) * NC
        for f in range(NC):
            for r in range(NY):
                source = ((y + NY - r) % NY) * (NZ * NC) + at + (c + f) % NC
                start = f * msg + r * cap
                out4[source, 0:cap, :] = fin[k, 0, start:start + cap, :]

    def d_copy(r):
        return remote(
            dsend.at[r - 1], drecv.at[r - 1], d_s.at[r - 1], d_r.at[r - 1],
            dev(y=(y + NY - r) % NY),
        )

    def combine():
        def one(k, carry):
            for f in range(NC):
                m = k * NC + f
                expert = (y * NZ + (z + NZ - z_step(k)) % NZ) * NC + (c + f) % NC
                high, low = pairs(0, expert)
                at = pl.ds(pl.multiple_of(m * msg, 16), msg)
                pa[0, at, :] = high
                pa[1, at, :] = low
            return carry

        lax.fori_loop(0, NZ, one, 0)
        for m in range(1, NZ * NC):
            az_copy(m // NC, m % NC).wait_recv()
        arrived = arecv[...].reshape(total * cap, width)
        over_rows = (((0,), (0,)), ((), ()))
        value = lax.dot_general(
            pa[0], arrived, over_rows, preferred_element_type=F32
        )
        value += lax.dot_general(
            pa[1], arrived, over_rows, preferred_element_type=F32
        )
        for r in range(1, NY):
            dsend[r - 1] = value[r * tok:(r + 1) * tok].astype(BF16)
            d_copy(r).start()
        dense[...] = value[:tok]

    def step(t, carry):
        def at(s, run):
            @pl.when((t >= s) & (t < s + blocks))
            def _():
                run(t - s)

        at(half * LAG + SWAP_LAG, finish)
        at(half * LAG, collect)
        for s in range(half - 1, 0, -1):
            at(s * LAG, functools.partial(pass_on, s=s))

        @pl.when((t > 0) & (t < blocks))
        def _():
            product(t)

        @pl.when(t == SEND_A)
        def _():
            for m in range(1, NZ * NC):
                az_copy(m // NC, m % NC).start()

        @pl.when(t == COMBINE_A)
        def _():
            combine()

        return carry

    lax.fori_loop(1, 3, fill_step, 0)
    product(0)
    lax.fori_loop(3, NZ, fill_step, 0)
    lax.fori_loop(0, blocks + half * LAG + SWAP_LAG, step, 0)

    for i in range(total):
        gout[i * cap:(i + 1) * cap, :] = out4[i, 0:cap, :]
    grad_ref[...] = gout[...].astype(BF16)

    result = dense[...]
    for r in range(1, NY):
        d_copy(r).wait_recv()
        result += drecv[r - 1].astype(F32)
    mixed_ref[...] = result.astype(BF16)

    for d in range(1, NY):
        y_copy(d).wait_send()
        d_copy(d).wait_send()

    def sent_z(m, carry):
        for f in range(NC):
            if f == 0:
                @pl.when(m > 0)
                def _():
                    bz_copy(m, 0).wait_send()
                    az_copy(m, 0).wait_send()
            else:
                bz_copy(m, f).wait_send()
                az_copy(m, f).wait_send()
        for s in range(half):
            plus(m, s).wait_send()
            minus(m, s).wait_send()
        swap(m).wait_send()
        return carry

    lax.fori_loop(0, NZ, sent_z, 0)


def on_device(hidden_a, expert_weights, routes_a, gates_a, cotangent_b, routes_b, gates_b):
    total = NY * NZ * NC
    _, slots, ff = hidden_a.shape
    cap = slots // total
    tok, width = cotangent_b.shape
    wide = -(-width // 128) * 128
    half, msg, block = NX // 2, NY * cap, NY * cap * NC
    count = NZ * NC
    vm, dma = pltpu.VMEM, pltpu.SemaphoreType.DMA
    whole = pl.BlockSpec(memory_space=pltpu.VMEM)
    anywhere = pl.BlockSpec(memory_space=pl.ANY)
    mixed, grad = pl.pallas_call(
        functools.partial(body, cap),
        out_shape=(
            jax.ShapeDtypeStruct((tok, width), BF16),
            jax.ShapeDtypeStruct((slots, 128), BF16),
        ),
        in_specs=[anywhere, anywhere] + [whole] * 5,
        out_specs=(whole, whole),
        scratch_shapes=[
            vm((slots, ff), BF16),
            vm((width, ff), BF16),
            vm((NY, tok, wide), BF16),
            vm((2, 3, 8, NY * tok), F32),
            vm((total, 16, width), F32),
            vm((msg, width), F32),
            vm((count, msg, width), BF16),
            vm((count, msg, width), BF16),
            vm((count, msg, width), BF16),
            vm((count, msg, width), BF16),
            vm((2, slots, NY * tok), BF16),
            vm((NZ, NX, 2, block, 128), F32),
            vm((NZ, half, 2, block, 128), BF16),
            vm((NZ, half, 2, block, 128), BF16),
            vm((NZ, half, 2, block, 128), BF16),
            vm((NZ, half, 2, block, 128), BF16),
            vm((NZ, 2, block, 128), F32),
            vm((NZ, block, 128), BF16),
            vm((NZ, block, 128), BF16),
            vm((total, 16, 128), F32),
            vm((slots, 128), F32),
            vm((tok, width), F32),
            vm((NY - 1, tok, width), BF16),
            vm((NY - 1, tok, width), BF16),
            dma((2,)),
            dma((NY - 1,)), dma((NY - 1,)),
            dma((count,)), dma((count,)),
            dma((count,)), dma((count,)),
            dma((NZ, half)), dma((NZ, half)),
            dma((NZ, half)), dma((NZ, half)),
            dma((NZ,)), dma((NZ,)),
            dma((NY - 1,)), dma((NY - 1,)),
        ],
        compiler_params=pltpu.CompilerParams(
            collective_id=0, has_side_effects=True,
            vmem_limit_bytes=56 * 1024 * 1024,
        ),
    )(
        hidden_a.reshape(slots, ff), expert_weights.reshape(ff, width).T,
        routes_a.T, gates_a.T, cotangent_b, routes_b.T, gates_b.T,
    )
    return mixed, grad.reshape(1, slots, 128)


def solution(mesh):
    in_specs = (
        P("expert", None, None),
        P("expert", None, "pipe"),
        P("expert", None),
        P("expert", None),
        P("expert", "pipe"),
        P("expert", None),
        P("expert", None),
    )
    out_specs = (P("expert", "pipe"), P("expert", None, "pipe"))
    return jax.shard_map(
        on_device, mesh=mesh, in_specs=in_specs, out_specs=out_specs, check_vma=False
    )
```

```python
import functools

import jax
import jax.numpy as jnp
from jax import lax
from jax.experimental import pallas as pl
from jax.experimental.pallas import tpu as pltpu
from jax.sharding import PartitionSpec as P

NX, NYH = 8, 2
NY, NZ, NC = 4, 8, 2
EARLY_A, SEND_A, COMBINE_A = 7, 2, 10
TRADE = 2
LAG, SWAP_LAG = 2, 3

BF16, F32 = jnp.bfloat16, jnp.float32


def body(
    cap,
    h_hbm, w_hbm, ra_hbm, ga_hbm, cot_hbm, rb_hbm, gb_hbm,
    mixed_ref, grad_ref,
    ra_ref, ga_ref, cot_ref, rb_ref, gb_ref, h_vm, w_vm, gath, codes, fwd, tile48, asend, arecv, bsend, brecv, pa,
    pbuf, splus, sminus, rplus, rminus, fin, hsend, hrecv, out4, gout,
    dense, dsend, drecv, both, tsend, trecv,
    load_sem, y_s, y_r, az_s, az_r, bz_s, bz_r, xp_s, xp_r, xm_s, xm_r,
    h_s, h_r, d_s, d_r, t_s, t_r,
):
    tok, width = cot_ref.shape
    top = ra_ref.shape[0]
    total = NY * NZ * NC
    msg = NY * cap
    half = NX // 2
    wide = gath.shape[2]
    p = lax.axis_index("pipe")
    e = lax.axis_index("expert")
    x, yh = p // NYH, p % NYH
    y, z, c = e // (NZ * NC), (e // NC) % NZ, e % NC

    def dev(x=x, yh=yh, y=y, z=z, c=c):
        return {"pipe": x * NYH + yh, "expert": (y * NZ + z) * NC + c}

    def z_step(k):
        if isinstance(k, int):
            return (k + 1) // 2 if k % 2 else (NZ - k // 2) % NZ
        return lax.select(k % 2 == 1, (k + 1) // 2, (NZ - k // 2) % NZ)

    def remote(src, dst, send, recv, to):
        return pltpu.make_async_remote_copy(
            src_ref=src, dst_ref=dst, send_sem=send, recv_sem=recv,
            device_id=to, device_id_type=pl.DeviceIdType.MESH,
        )

    load_w = pltpu.make_async_copy(w_hbm, w_vm, load_sem.at[0])
    load_h = pltpu.make_async_copy(h_hbm, h_vm, load_sem.at[1])
    partners = [dev(y=(y + d) % NY) for d in range(1, NY)]
    partners += [
        dev(z=(z + d) % NZ, c=(c + f) % NC)
        for d in range(NZ) for f in range(NC) if d or f
    ]
    partners += [dev(x=(x + 1) % NX), dev(x=(x + NX - 1) % NX), dev(yh=1 - yh)]
    barrier = pltpu.get_barrier_semaphore()
    for to in partners:
        pl.semaphore_signal(
            barrier, inc=1, device_id=to, device_id_type=pl.DeviceIdType.MESH
        )
    small = [
        pltpu.make_async_copy(src, dst, load_sem.at[2 + n])
        for n, (src, dst) in enumerate((
            (ra_hbm, ra_ref), (ga_hbm, ga_ref), (rb_hbm, rb_ref),
            (gb_hbm, gb_ref), (cot_hbm, cot_ref),
        ))
    ]
    for copy in small:
        copy.start()
    load_w.start()
    load_h.start()
    for copy in small:
        copy.wait()

    base = width - (wide - 128)

    def mask(test, shape):
        rows = lax.broadcasted_iota(jnp.int32, shape, 0)
        cols = lax.broadcasted_iota(jnp.int32, shape, 1)
        return test(rows, cols).astype(F32).astype(BF16)

    after = mask(lambda i, j: i < j, (tok, tok))
    expert_row = lax.broadcasted_iota(jnp.int32, (total, tok), 0)
    notes = []
    for r_ref, g_ref in ((ra_ref, ga_ref), (rb_ref, gb_ref)):
        routes = r_ref[...]
        gates = g_ref[...]
        high = gates.astype(BF16)
        low = (gates - high.astype(F32)).astype(BF16)
        hit = [routes[k:k + 1, :] == expert_row for k in range(top)]
        member = jnp.zeros((total, tok), F32)
        for k in range(top):
            member = jnp.where(hit[k], 1.0, member)
        rank = jnp.dot(member.astype(BF16), after, preferred_element_type=F32)
        slot = [
            jnp.sum(jnp.where(hit[k], rank, 0.0), axis=0, keepdims=True)
            for k in range(top)
        ]
        notes += [routes.astype(F32), jnp.concatenate(slot, axis=0)]
        notes += [high.astype(F32), low.astype(F32)]
    tail = jnp.dot(
        cot_ref[:, wide - 128:], mask(lambda i, j: i == j, (base, 128)),
        preferred_element_type=F32,
    )
    tail += jnp.dot(
        jnp.concatenate(notes, axis=0).astype(BF16),
        mask(lambda i, j: i + base == j, (tok, 128)),
        preferred_element_type=F32,
    )
    gath[0, :, :wide - 128] = cot_ref[:, :wide - 128]
    gath[0, :, wide - 128:] = tail.astype(BF16)

    pl.semaphore_wait(barrier, len(partners))

    def y_copy(d):
        return remote(
            gath.at[0], gath.at[d], y_s.at[d - 1], y_r.at[d - 1],
            dev(y=(y + d) % NY),
        )

    for d in (2, 1, 3):
        if d < NY:
            y_copy(d).start()

    load_w.wait()
    load_h.wait()
    rows = NZ * NC * cap

    def forward(j, carry):
        value = lax.dot_general(
            h_vm[pl.ds(pl.multiple_of(j * rows, 16), rows), :], w_vm[...],
            (((1,), (1,)), ((), ())), preferred_element_type=F32,
        )
        for i in range(NZ * NC):
            fwd[j * (NZ * NC) + i, 0:cap, :] = value[i * cap:(i + 1) * cap, :]
        return carry

    lax.fori_loop(0, NY, forward, 0)

    def pack_a(k, carry):
        to = ((z + z_step(k)) % NZ) * NC
        for f in range(NC):
            for r in range(NY):
                source = ((y + NY - r) % NY) * (NZ * NC) + to + (c + f) % NC
                tile48[r * cap:(r + 1) * cap, :] = fwd[source, 0:cap, :]
            asend[k * NC + f] = tile48[...].astype(BF16)
        return carry

    lax.fori_loop(0, NZ, pack_a, 0)
    arecv[0] = asend[0]

    def az_copy(k, f):
        m = k * NC + f
        return remote(
            asend.at[m], arecv.at[m], az_s.at[m], az_r.at[m],
            dev(z=(z + z_step(k)) % NZ, c=(c + f) % NC),
        )

    def send_a(first, last):
        def one(k, carry):
            for f in range(NC):
                az_copy(k, f).start()
            return carry

        lax.fori_loop(first, last, one, 0)

    send_a(EARLY_A, NZ)

    for d in range(1, NY):
        y_copy(d).wait_recv()

    for r in range(0, NY, 2):
        left = pltpu.roll(gath[r, :, wide - 128:].astype(F32), 128 - base, 1)
        right = gath[r + 1, :, wide - 128:].astype(F32)
        lane = lax.broadcasted_iota(jnp.int32, (tok, 128), 1)
        info = jnp.where(lane < tok, left, right)
        cols = slice(r * tok, (r + 2) * tok)
        for n in range(2):
            at = n * 4 * 8
            codes[n, 0, :, cols] = info[at:at + 8] * 16.0 + info[at + 8:at + 16]
            codes[n, 1, :, cols] = info[at + 16:at + 24]
            codes[n, 2, :, cols] = info[at + 24:at + 32]

    row = lax.broadcasted_iota(jnp.int32, (msg, NY * tok), 0)
    col = lax.broadcasted_iota(jnp.int32, (msg, NY * tok), 1)
    slot_code = jnp.full((msg, NY * tok), -4096.0, F32)
    for r in range(NY):
        inside = (
            (row >= r * cap) & (row < (r + 1) * cap)
            & (col >= r * tok) & (col < (r + 1) * tok)
        )
        slot_code = jnp.where(inside, (row - r * cap).astype(F32), slot_code)

    def pairs(n, expert):
        want = slot_code + (expert * 16).astype(F32)
        high = jnp.zeros((msg, NY * tok), F32)
        low = jnp.zeros((msg, NY * tok), F32)
        for k in range(top):
            same = want == codes[n, 0, k:k + 1, :]
            high = jnp.where(same, codes[n, 1, k:k + 1, :], high)
            low = jnp.where(same, codes[n, 2, k:k + 1, :], low)
        return high.astype(BF16), low.astype(BF16)

    def bz_copy(k, f):
        m = k * NC + f
        return remote(
            bsend.at[m], brecv.at[m], bz_s.at[m], bz_r.at[m],
            dev(z=(z + z_step(k)) % NZ, c=(c + f) % NC),
        )

    def fill(k, f):
        expert = (y * NZ + (z + z_step(k)) % NZ) * NC + (c + f) % NC
        high, low = pairs(1, expert)
        cots = gath[...].reshape(NY * tok, wide)
        value = jnp.dot(
            jnp.concatenate([high, low], axis=0), cots, preferred_element_type=F32
        )
        return (value[:msg, :width] + value[msg:, :width]).astype(BF16)

    for f in range(1, NC):
        bsend[f] = fill(0, f)
        bz_copy(0, f).start()
    brecv[0] = fill(0, 0)

    def fill_step(k, carry):
        for f in range(NC):
            bsend[k * NC + f] = fill(k, f)
            bz_copy(k, f).start()
        return carry

    block = NC * msg
    blocks = NZ

    def plus(k, s):
        to, sems = dev(x=(x + 1) % NX), (xp_s.at[k, s], xp_r.at[k, s])
        if s == 0:
            return remote(splus.at[k, s, 0], rplus.at[k, s, 0], *sems, to)
        return remote(splus.at[k, s], rplus.at[k, s], *sems, to)

    def minus(k, s):
        to, sems = dev(x=(x + NX - 1) % NX), (xm_s.at[k, s], xm_r.at[k, s])
        if s == 0:
            return remote(sminus.at[k, s, 1], rminus.at[k, s, 1], *sems, to)
        return remote(sminus.at[k, s], rminus.at[k, s], *sems, to)

    def swap(k):
        return remote(
            hsend.at[k], hrecv.at[k], h_s.at[k], h_r.at[k], dev(yh=1 - yh)
        )

    def trade():
        return remote(tsend, trecv, t_s, t_r, dev(yh=1 - yh))

    def at_step(p):
        return lax.select(p == 0, 0, lax.select(p == blocks - 1, 1, p + 1))

    def traded_product():
        for f in range(NC):
            bz_copy(1, f).wait_recv()
        value = brecv[NC:2 * NC].reshape(block, width)
        for off in range(NX):
            q = (x + off) % NX
            part = jnp.dot(
                value, w_vm[:, pl.ds(pl.multiple_of(q * 256, 256), 256)],
                preferred_element_type=F32,
            )
            both[0] = part[:, :128]
            both[1] = part[:, 128:]
            tsend[off] = both[1 - yh].astype(BF16)
            pbuf[1, off, 0] = both[yh]
        trade().start()

    def traded_plus(s):
        return remote(
            splus.at[1, s, 0], rplus.at[1, s, 0], xp_s.at[1, s], xp_r.at[1, s],
            dev(x=(x + 1) % NX),
        )

    def traded_minus(s):
        return remote(
            sminus.at[1, s, 0], rminus.at[1, s, 0], xm_s.at[1, s], xm_r.at[1, s],
            dev(x=(x + NX - 1) % NX),
        )

    def traded_first():
        trade().wait_recv()
        for off in [half] + [i for i in range(NX) if i != half]:
            value = pbuf[1, off, 0] + trecv[off].astype(F32)
            if off == half:
                splus[1, 0, 0] = value.astype(BF16)
                traded_plus(0).start()
            else:
                pbuf[1, off, 0] = value

    def traded_pass(s):
        traded_plus(s - 1).wait_recv()
        value = pbuf[1, half - s, 0] + rplus[1, s - 1, 0].astype(F32)
        splus[1, s, 0] = value.astype(BF16)
        traded_plus(s).start()
        value = pbuf[1, half + s, 0]
        if s > 1:
            traded_minus(s - 1).wait_recv()
            value += rminus[1, s - 1, 0].astype(F32)
        sminus[1, s, 0] = value.astype(BF16)
        traded_minus(s).start()

    def scatter(k):
        at = ((z + NZ - z_step(k)) % NZ) * NC
        for f in range(NC):
            for r in range(NY):
                source = ((y + NY - r) % NY) * (NZ * NC) + at + (c + f) % NC
                start = f * msg + r * cap
                out4[source, 0:cap, :] = fin[k, 0, start:start + cap, :]

    def traded_collect():
        traded_plus(half - 1).wait_recv()
        traded_minus(half - 1).wait_recv()
        value = pbuf[1, 0, 0] + rplus[1, half - 1, 0].astype(F32)
        fin[1, 0] = value + rminus[1, half - 1, 0].astype(F32)
        scatter(1)

    def product(k):
        if isinstance(k, int):
            for f in range(1, NC):
                bz_copy(k, f).wait_recv()
        else:
            for f in range(NC):
                bz_copy(k, f).wait_recv()
        value = brecv[pl.ds(k * NC, NC)].reshape(block, width)
        order = [half]
        for i in range(half - 1, 0, -1):
            order += [i, NX - i]
        for off in order + [0]:
            q = (x + off) % NX
            part = jnp.dot(
                value, w_vm[:, pl.ds(pl.multiple_of(q * 256, 256), 256)],
                preferred_element_type=F32,
            )
            if off == half:
                splus[k, 0, 0] = part[:, :128].astype(BF16)
                plus(k, 0).start()
                sminus[k, 0, 1] = part[:, 128:].astype(BF16)
                minus(k, 0).start()
            else:
                pbuf[k, off, 0] = part[:, :128]
                pbuf[k, off, 1] = part[:, 128:]

    def pass_on(k, s):
        plus(k, s - 1).wait_recv()
        for h in range(2):
            value = pbuf[k, half - s, h]
            if s > 1 or h == 0:
                value += rplus[k, s - 1, h].astype(F32)
            splus[k, s, h] = value.astype(BF16)
        plus(k, s).start()
        minus(k, s - 1).wait_recv()
        for h in range(2):
            value = pbuf[k, half + s, h]
            if s > 1 or h == 1:
                value += rminus[k, s - 1, h].astype(F32)
            sminus[k, s, h] = value.astype(BF16)
        minus(k, s).start()

    def collect(k):
        plus(k, half - 1).wait_recv()
        minus(k, half - 1).wait_recv()
        for h in range(2):
            value = pbuf[k, 0, h] + rplus[k, half - 1, h].astype(F32)
            fin[k, h] = value + rminus[k, half - 1, h].astype(F32)
        hsend[k] = fin[k, 1 - yh].astype(BF16)
        swap(k).start()

    def finish(k):
        swap(k).wait_recv()
        fin[k, 0] = fin[k, yh] + hrecv[k].astype(F32)
        scatter(k)

    def d_copy(r):
        return remote(
            dsend.at[r - 1], drecv.at[r - 1], d_s.at[r - 1], d_r.at[r - 1],
            dev(y=(y + NY - r) % NY),
        )

    def rows_a(k):
        for f in range(NC):
            m = k * NC + f
            expert = (y * NZ + (z + NZ - z_step(k)) % NZ) * NC + (c + f) % NC
            high, low = pairs(0, expert)
            at = pl.ds(pl.multiple_of(m * msg, 16), msg)
            pa[0, at, :] = high
            pa[1, at, :] = low

    def combine():
        for m in range(1, NZ * NC):
            az_copy(m // NC, m % NC).wait_recv()
        arrived = arecv[...].reshape(total * cap, width)
        over_rows = (((0,), (0,)), ((), ()))
        value = lax.dot_general(
            pa[0], arrived, over_rows, preferred_element_type=F32
        )
        value += lax.dot_general(
            pa[1], arrived, over_rows, preferred_element_type=F32
        )
        for r in range(1, NY):
            dsend[r - 1] = value[r * tok:(r + 1) * tok].astype(BF16)
            d_copy(r).start()
        dense[...] = value[:tok]

    def step(t, carry):
        def at(s, run):
            @pl.when((t >= s) & (t < s + blocks - 1))
            def _():
                run(at_step(t - s))

        def last(s, run):
            @pl.when(t == s + blocks - 1)
            def _():
                run()

        at(half * LAG + SWAP_LAG, finish)
        at(half * LAG, collect)
        last(half * LAG, traded_collect)
        for s in range(half - 1, 0, -1):
            at(s * LAG, functools.partial(pass_on, s=s))
            last(s * LAG, functools.partial(traded_pass, s))

        last(0, traded_first)

        @pl.when((t > 0) & (t < blocks - 1))
        def _():
            product(at_step(t))

        @pl.when(t == TRADE)
        def _():
            traded_product()

        @pl.when((t >= 1) & (t <= NZ))
        def _():
            rows_a(t - 1)

        @pl.when(t == SEND_A)
        def _():
            for f in range(1, NC):
                az_copy(0, f).start()
            send_a(1, EARLY_A)

        @pl.when(t == COMBINE_A)
        def _():
            combine()

        return carry

    lax.fori_loop(1, 3, fill_step, 0)
    product(0)
    lax.fori_loop(3, NZ, fill_step, 0)
    lax.fori_loop(0, blocks + half * LAG + SWAP_LAG, step, 0)

    for i in range(total):
        gout[i * cap:(i + 1) * cap, :] = out4[i, 0:cap, :]
    grad_ref[...] = gout[...].astype(BF16)

    result = dense[...]
    for r in range(1, NY):
        d_copy(r).wait_recv()
        result += drecv[r - 1].astype(F32)
    mixed_ref[...] = result.astype(BF16)

    for d in range(1, NY):
        y_copy(d).wait_send()
        d_copy(d).wait_send()

    def sent_z(m, carry):
        for f in range(NC):
            if f == 0:
                @pl.when(m > 0)
                def _():
                    bz_copy(m, 0).wait_send()
                    az_copy(m, 0).wait_send()
            else:
                bz_copy(m, f).wait_send()
                az_copy(m, f).wait_send()
        @pl.when(m != 1)
        def _():
            for s in range(half):
                plus(m, s).wait_send()
                minus(m, s).wait_send()
            swap(m).wait_send()

        return carry

    lax.fori_loop(0, NZ, sent_z, 0)
    trade().wait_send()
    for s in range(half):
        traded_plus(s).wait_send()
        if s:
            traded_minus(s).wait_send()


def write(mixed_in, grad_in, mixed_out, grad_out):
    mixed_out[...] = mixed_in[...]
    grad_out[...] = grad_in[...]


def on_device(hidden_a, expert_weights, routes_a, gates_a, cotangent_b, routes_b, gates_b):
    total = NY * NZ * NC
    _, slots, ff = hidden_a.shape
    cap = slots // total
    tok, width = cotangent_b.shape
    wide = -(-width // 128) * 128
    half, msg, block = NX // 2, NY * cap, NY * cap * NC
    count = NZ * NC
    vm, dma = pltpu.VMEM, pltpu.SemaphoreType.DMA
    whole = pl.BlockSpec(memory_space=pltpu.VMEM)
    anywhere = pl.BlockSpec(memory_space=pl.ANY)
    mixed, grad = pl.pallas_call(
        functools.partial(body, cap),
        out_shape=(
            jax.ShapeDtypeStruct((tok, width), BF16),
            jax.ShapeDtypeStruct((slots, 128), BF16),
        ),
        in_specs=[anywhere] * 7,
        out_specs=(whole, whole),
        scratch_shapes=[
            vm(routes_a.T.shape, routes_a.dtype),
            vm(gates_a.T.shape, F32),
            vm((tok, width), BF16),
            vm(routes_b.T.shape, routes_b.dtype),
            vm(gates_b.T.shape, F32),
            vm((slots, ff), BF16),
            vm((width, ff), BF16),
            vm((NY, tok, wide), BF16),
            vm((2, 3, 8, NY * tok), F32),
            vm((total, 16, width), F32),
            vm((msg, width), F32),
            vm((count, msg, width), BF16),
            vm((count, msg, width), BF16),
            vm((count, msg, width), BF16),
            vm((count, msg, width), BF16),
            vm((2, slots, NY * tok), BF16),
            vm((NZ, NX, 2, block, 128), F32),
            vm((NZ, half, 2, block, 128), BF16),
            vm((NZ, half, 2, block, 128), BF16),
            vm((NZ, half, 2, block, 128), BF16),
            vm((NZ, half, 2, block, 128), BF16),
            vm((NZ, 2, block, 128), F32),
            vm((NZ, block, 128), BF16),
            vm((NZ, block, 128), BF16),
            vm((total, 16, 128), F32),
            vm((slots, 128), F32),
            vm((tok, width), F32),
            vm((NY - 1, tok, width), BF16),
            vm((NY - 1, tok, width), BF16),
            vm((2, block, 128), F32),
            vm((NX, block, 128), BF16),
            vm((NX, block, 128), BF16),
            dma((7,)),
            dma((NY - 1,)), dma((NY - 1,)),
            dma((count,)), dma((count,)),
            dma((count,)), dma((count,)),
            dma((NZ, half)), dma((NZ, half)),
            dma((NZ, half)), dma((NZ, half)),
            dma((NZ,)), dma((NZ,)),
            dma((NY - 1,)), dma((NY - 1,)), dma, dma,
        ],
        compiler_params=pltpu.CompilerParams(
            collective_id=0, has_side_effects=True,
            vmem_limit_bytes=56 * 1024 * 1024,
        ),
    )(
        hidden_a.reshape(slots, ff), expert_weights.reshape(ff, width).T,
        routes_a.T, gates_a.T, cotangent_b, routes_b.T, gates_b.T,
    )
    mixed, grad = pl.pallas_call(
        write,
        out_shape=(
            jax.ShapeDtypeStruct((tok, width), BF16),
            jax.ShapeDtypeStruct((slots, 128), BF16),
        ),
        in_specs=[whole, whole],
        out_specs=(whole, whole),
    )(mixed, grad)
    return mixed, grad.reshape(1, slots, 128)


def solution(mesh):
    in_specs = (
        P("expert", None, None),
        P("expert", None, "pipe"),
        P("expert", None),
        P("expert", None),
        P("expert", "pipe"),
        P("expert", None),
        P("expert", None),
    )
    out_specs = (P("expert", "pipe"), P("expert", None, "pipe"))
    return jax.shard_map(
        on_device, mesh=mesh, in_specs=in_specs, out_specs=out_specs, check_vma=False
    )
```

```python
import functools

import jax
import jax.numpy as jnp
from jax import lax
from jax.experimental import pallas as pl
from jax.experimental.pallas import tpu as pltpu
from jax.sharding import PartitionSpec as P

NX, NYH = 8, 2
NY, NZ, NC = 4, 8, 2
EARLY_A, SEND_A, COMBINE_A = 7, 1, 9
TRADE = 2
LAG, SWAP_LAG = 2, 3

BF16, F32 = jnp.bfloat16, jnp.float32


def body(
    cap,
    h_hbm, w_hbm, ra_hbm, ga_hbm, cot_hbm, rb_hbm, gb_hbm,
    mixed_ref, grad_ref,
    ra_ref, ga_ref, cot_ref, rb_ref, gb_ref, h_vm, w_vm, gath, codes, fwd, tile48, asend, arecv, bsend, brecv, pa,
    pbuf, splus, sminus, rplus, rminus, fin, hsend, hrecv, out4, gout,
    dense, dsend, drecv, both, tsend, trecv,
    load_sem, y_s, y_r, az_s, az_r, bz_s, bz_r, xp_s, xp_r, xm_s, xm_r,
    h_s, h_r, d_s, d_r, t_s, t_r,
):
    tok, width = cot_ref.shape
    top = ra_ref.shape[0]
    total = NY * NZ * NC
    msg = NY * cap
    half = NX // 2
    wide = gath.shape[2]
    p = lax.axis_index("pipe")
    e = lax.axis_index("expert")
    x, yh = p // NYH, p % NYH
    y, z, c = e // (NZ * NC), (e // NC) % NZ, e % NC

    def dev(x=x, yh=yh, y=y, z=z, c=c):
        return {"pipe": x * NYH + yh, "expert": (y * NZ + z) * NC + c}

    def z_step(k):
        if isinstance(k, int):
            return (k + 1) // 2 if k % 2 else (NZ - k // 2) % NZ
        return lax.select(k % 2 == 1, (k + 1) // 2, (NZ - k // 2) % NZ)

    def remote(src, dst, send, recv, to):
        return pltpu.make_async_remote_copy(
            src_ref=src, dst_ref=dst, send_sem=send, recv_sem=recv,
            device_id=to, device_id_type=pl.DeviceIdType.MESH,
        )

    load_w = pltpu.make_async_copy(w_hbm, w_vm, load_sem.at[0])
    load_h = pltpu.make_async_copy(h_hbm, h_vm, load_sem.at[1])
    partners = [dev(y=(y + d) % NY) for d in range(1, NY)]
    partners += [
        dev(z=(z + d) % NZ, c=(c + f) % NC)
        for d in range(NZ) for f in range(NC) if d or f
    ]
    partners += [dev(x=(x + 1) % NX), dev(x=(x + NX - 1) % NX), dev(yh=1 - yh)]
    barrier = pltpu.get_barrier_semaphore()
    for to in partners:
        pl.semaphore_signal(
            barrier, inc=1, device_id=to, device_id_type=pl.DeviceIdType.MESH
        )
    small = [
        pltpu.make_async_copy(src, dst, load_sem.at[2 + n])
        for n, (src, dst) in enumerate((
            (ra_hbm, ra_ref), (ga_hbm, ga_ref), (rb_hbm, rb_ref),
            (gb_hbm, gb_ref), (cot_hbm, cot_ref),
        ))
    ]
    for copy in small:
        copy.start()
    load_w.start()
    load_h.start()
    for copy in small:
        copy.wait()

    base = width - (wide - 128)

    def mask(test, shape):
        rows = lax.broadcasted_iota(jnp.int32, shape, 0)
        cols = lax.broadcasted_iota(jnp.int32, shape, 1)
        return test(rows, cols).astype(F32).astype(BF16)

    after = mask(lambda i, j: i < j, (tok, tok))
    expert_row = lax.broadcasted_iota(jnp.int32, (total, tok), 0)
    notes = []
    for r_ref, g_ref in ((ra_ref, ga_ref), (rb_ref, gb_ref)):
        routes = r_ref[...]
        gates = g_ref[...]
        high = gates.astype(BF16)
        low = (gates - high.astype(F32)).astype(BF16)
        hit = [routes[k:k + 1, :] == expert_row for k in range(top)]
        member = jnp.zeros((total, tok), F32)
        for k in range(top):
            member = jnp.where(hit[k], 1.0, member)
        rank = jnp.dot(member.astype(BF16), after, preferred_element_type=F32)
        slot = [
            jnp.sum(jnp.where(hit[k], rank, 0.0), axis=0, keepdims=True)
            for k in range(top)
        ]
        notes += [routes.astype(F32), jnp.concatenate(slot, axis=0)]
        notes += [high.astype(F32), low.astype(F32)]
    tail = jnp.dot(
        cot_ref[:, wide - 128:], mask(lambda i, j: i == j, (base, 128)),
        preferred_element_type=F32,
    )
    tail += jnp.dot(
        jnp.concatenate(notes, axis=0).astype(BF16),
        mask(lambda i, j: i + base == j, (tok, 128)),
        preferred_element_type=F32,
    )
    gath[0, :, :wide - 128] = cot_ref[:, :wide - 128]
    gath[0, :, wide - 128:] = tail.astype(BF16)

    pl.semaphore_wait(barrier, len(partners))

    def y_copy(d):
        return remote(
            gath.at[0], gath.at[d], y_s.at[d - 1], y_r.at[d - 1],
            dev(y=(y + d) % NY),
        )

    for d in (2, 1, 3):
        if d < NY:
            y_copy(d).start()

    load_w.wait()
    load_h.wait()
    rows = NZ * NC * cap

    def forward(j, carry):
        value = lax.dot_general(
            h_vm[pl.ds(pl.multiple_of(j * rows, 16), rows), :], w_vm[...],
            (((1,), (1,)), ((), ())), preferred_element_type=F32,
        )
        for i in range(NZ * NC):
            fwd[j * (NZ * NC) + i, 0:cap, :] = value[i * cap:(i + 1) * cap, :]
        return carry

    lax.fori_loop(0, NY, forward, 0)

    def pack_a(k, carry):
        to = ((z + z_step(k)) % NZ) * NC
        for f in range(NC):
            for r in range(NY):
                source = ((y + NY - r) % NY) * (NZ * NC) + to + (c + f) % NC
                tile48[r * cap:(r + 1) * cap, :] = fwd[source, 0:cap, :]
            asend[k * NC + f] = tile48[...].astype(BF16)
        return carry

    lax.fori_loop(0, NZ, pack_a, 0)
    arecv[0] = asend[0]

    def az_copy(k, f):
        m = k * NC + f
        return remote(
            asend.at[m], arecv.at[m], az_s.at[m], az_r.at[m],
            dev(z=(z + z_step(k)) % NZ, c=(c + f) % NC),
        )

    def send_a(first, last):
        def one(k, carry):
            for f in range(NC):
                az_copy(k, f).start()
            return carry

        lax.fori_loop(first, last, one, 0)

    send_a(EARLY_A, NZ)

    for d in range(1, NY):
        y_copy(d).wait_recv()

    for r in range(0, NY, 2):
        left = pltpu.roll(gath[r, :, wide - 128:].astype(F32), 128 - base, 1)
        right = gath[r + 1, :, wide - 128:].astype(F32)
        lane = lax.broadcasted_iota(jnp.int32, (tok, 128), 1)
        info = jnp.where(lane < tok, left, right)
        cols = slice(r * tok, (r + 2) * tok)
        for n in range(2):
            at = n * 4 * 8
            codes[n, 0, :, cols] = info[at:at + 8] * 16.0 + info[at + 8:at + 16]
            codes[n, 1, :, cols] = info[at + 16:at + 24]
            codes[n, 2, :, cols] = info[at + 24:at + 32]

    row = lax.broadcasted_iota(jnp.int32, (msg, NY * tok), 0)
    col = lax.broadcasted_iota(jnp.int32, (msg, NY * tok), 1)
    slot_code = jnp.full((msg, NY * tok), -4096.0, F32)
    for r in range(NY):
        inside = (
            (row >= r * cap) & (row < (r + 1) * cap)
            & (col >= r * tok) & (col < (r + 1) * tok)
        )
        slot_code = jnp.where(inside, (row - r * cap).astype(F32), slot_code)

    def pairs(n, expert):
        want = slot_code + (expert * 16).astype(F32)
        high = jnp.zeros((msg, NY * tok), F32)
        low = jnp.zeros((msg, NY * tok), F32)
        for k in range(top):
            same = want == codes[n, 0, k:k + 1, :]
            high = jnp.where(same, codes[n, 1, k:k + 1, :], high)
            low = jnp.where(same, codes[n, 2, k:k + 1, :], low)
        return high.astype(BF16), low.astype(BF16)

    def bz_copy(k, f):
        m = k * NC + f
        return remote(
            bsend.at[m], brecv.at[m], bz_s.at[m], bz_r.at[m],
            dev(z=(z + z_step(k)) % NZ, c=(c + f) % NC),
        )

    def fill(k, f):
        expert = (y * NZ + (z + z_step(k)) % NZ) * NC + (c + f) % NC
        high, low = pairs(1, expert)
        cots = gath[...].reshape(NY * tok, wide)
        value = jnp.dot(
            jnp.concatenate([high, low], axis=0), cots, preferred_element_type=F32
        )
        return (value[:msg, :width] + value[msg:, :width]).astype(BF16)

    for f in range(1, NC):
        bsend[f] = fill(0, f)
        bz_copy(0, f).start()
    brecv[0] = fill(0, 0)

    def fill_step(k, carry):
        for f in range(NC):
            bsend[k * NC + f] = fill(k, f)
            bz_copy(k, f).start()
        return carry

    block = NC * msg
    blocks = NZ

    def plus(k, s):
        to, sems = dev(x=(x + 1) % NX), (xp_s.at[k, s], xp_r.at[k, s])
        if s == 0:
            return remote(splus.at[k, s, 0], rplus.at[k, s, 0], *sems, to)
        return remote(splus.at[k, s], rplus.at[k, s], *sems, to)

    def minus(k, s):
        to, sems = dev(x=(x + NX - 1) % NX), (xm_s.at[k, s], xm_r.at[k, s])
        if s == 0:
            return remote(sminus.at[k, s, 1], rminus.at[k, s, 1], *sems, to)
        return remote(sminus.at[k, s], rminus.at[k, s], *sems, to)

    def swap(k):
        return remote(
            hsend.at[k], hrecv.at[k], h_s.at[k], h_r.at[k], dev(yh=1 - yh)
        )

    def trade():
        return remote(tsend, trecv, t_s, t_r, dev(yh=1 - yh))

    def at_step(p):
        return lax.select(p == 0, 0, lax.select(p == blocks - 1, 1, p + 1))

    def traded_product():
        for f in range(NC):
            bz_copy(1, f).wait_recv()
        value = brecv[NC:2 * NC].reshape(block, width)
        for off in range(NX):
            q = (x + off) % NX
            part = jnp.dot(
                value, w_vm[:, pl.ds(pl.multiple_of(q * 256, 256), 256)],
                preferred_element_type=F32,
            )
            both[0] = part[:, :128]
            both[1] = part[:, 128:]
            tsend[off] = both[1 - yh].astype(BF16)
            pbuf[1, off, 0] = both[yh]
        trade().start()

    def traded_plus(s):
        return remote(
            splus.at[1, s, 0], rplus.at[1, s, 0], xp_s.at[1, s], xp_r.at[1, s],
            dev(x=(x + 1) % NX),
        )

    def traded_minus(s):
        return remote(
            sminus.at[1, s, 0], rminus.at[1, s, 0], xm_s.at[1, s], xm_r.at[1, s],
            dev(x=(x + NX - 1) % NX),
        )

    def traded_first():
        trade().wait_recv()
        for off in [half] + [i for i in range(NX) if i != half]:
            value = pbuf[1, off, 0] + trecv[off].astype(F32)
            if off == half:
                splus[1, 0, 0] = value.astype(BF16)
                traded_plus(0).start()
            else:
                pbuf[1, off, 0] = value

    def traded_pass(s):
        traded_plus(s - 1).wait_recv()
        value = pbuf[1, half - s, 0] + rplus[1, s - 1, 0].astype(F32)
        splus[1, s, 0] = value.astype(BF16)
        traded_plus(s).start()
        value = pbuf[1, half + s, 0]
        if s > 1:
            traded_minus(s - 1).wait_recv()
            value += rminus[1, s - 1, 0].astype(F32)
        sminus[1, s, 0] = value.astype(BF16)
        traded_minus(s).start()

    def scatter(k):
        at = ((z + NZ - z_step(k)) % NZ) * NC
        for f in range(NC):
            for r in range(NY):
                source = ((y + NY - r) % NY) * (NZ * NC) + at + (c + f) % NC
                start = f * msg + r * cap
                out4[source, 0:cap, :] = fin[k, 0, start:start + cap, :]

    def traded_collect():
        traded_plus(half - 1).wait_recv()
        traded_minus(half - 1).wait_recv()
        value = pbuf[1, 0, 0] + rplus[1, half - 1, 0].astype(F32)
        fin[1, 0] = value + rminus[1, half - 1, 0].astype(F32)
        scatter(1)

    def product(k):
        if isinstance(k, int):
            for f in range(1, NC):
                bz_copy(k, f).wait_recv()
        else:
            for f in range(NC):
                bz_copy(k, f).wait_recv()
        value = brecv[pl.ds(k * NC, NC)].reshape(block, width)
        order = [half]
        for i in range(half - 1, 0, -1):
            order += [i, NX - i]
        for off in order + [0]:
            q = (x + off) % NX
            part = jnp.dot(
                value, w_vm[:, pl.ds(pl.multiple_of(q * 256, 256), 256)],
                preferred_element_type=F32,
            )
            if off == half:
                splus[k, 0, 0] = part[:, :128].astype(BF16)
                plus(k, 0).start()
                sminus[k, 0, 1] = part[:, 128:].astype(BF16)
                minus(k, 0).start()
            else:
                pbuf[k, off, 0] = part[:, :128]
                pbuf[k, off, 1] = part[:, 128:]

    def pass_on(k, s):
        plus(k, s - 1).wait_recv()
        for h in range(2):
            value = pbuf[k, half - s, h]
            if s > 1 or h == 0:
                value += rplus[k, s - 1, h].astype(F32)
            splus[k, s, h] = value.astype(BF16)
        plus(k, s).start()
        minus(k, s - 1).wait_recv()
        for h in range(2):
            value = pbuf[k, half + s, h]
            if s > 1 or h == 1:
                value += rminus[k, s - 1, h].astype(F32)
            sminus[k, s, h] = value.astype(BF16)
        minus(k, s).start()

    def collect(k):
        plus(k, half - 1).wait_recv()
        minus(k, half - 1).wait_recv()
        for h in range(2):
            value = pbuf[k, 0, h] + rplus[k, half - 1, h].astype(F32)
            fin[k, h] = value + rminus[k, half - 1, h].astype(F32)
        hsend[k] = fin[k, 1 - yh].astype(BF16)
        swap(k).start()

    def finish(k):
        swap(k).wait_recv()
        fin[k, 0] = fin[k, yh] + hrecv[k].astype(F32)
        scatter(k)

    def d_copy(r):
        return remote(
            dsend.at[r - 1], drecv.at[r - 1], d_s.at[r - 1], d_r.at[r - 1],
            dev(y=(y + NY - r) % NY),
        )

    def rows_a(k):
        for f in range(NC):
            m = k * NC + f
            expert = (y * NZ + (z + NZ - z_step(k)) % NZ) * NC + (c + f) % NC
            high, low = pairs(0, expert)
            at = pl.ds(pl.multiple_of(m * msg, 16), msg)
            pa[0, at, :] = high
            pa[1, at, :] = low

    def combine():
        for m in range(1, NZ * NC):
            az_copy(m // NC, m % NC).wait_recv()
        arrived = arecv[...].reshape(total * cap, width)
        over_rows = (((0,), (0,)), ((), ()))
        value = lax.dot_general(
            pa[0], arrived, over_rows, preferred_element_type=F32
        )
        value += lax.dot_general(
            pa[1], arrived, over_rows, preferred_element_type=F32
        )
        for r in range(1, NY):
            dsend[r - 1] = value[r * tok:(r + 1) * tok].astype(BF16)
            d_copy(r).start()
        dense[...] = value[:tok]

    def step(t, carry):
        def at(s, run):
            @pl.when((t >= s) & (t < s + blocks - 1))
            def _():
                run(at_step(t - s))

        def last(s, run):
            @pl.when(t == s + blocks - 1)
            def _():
                run()

        at(half * LAG + SWAP_LAG, finish)
        at(half * LAG, collect)
        last(half * LAG, traded_collect)
        for s in range(half - 1, 0, -1):
            at(s * LAG, functools.partial(pass_on, s=s))
            last(s * LAG, functools.partial(traded_pass, s))

        last(0, traded_first)

        @pl.when((t > 0) & (t < blocks - 1))
        def _():
            product(at_step(t))

        @pl.when(t == TRADE)
        def _():
            traded_product()

        @pl.when((t >= 1) & (t <= NZ))
        def _():
            rows_a(t - 1)

        @pl.when(t == SEND_A)
        def _():
            for f in range(1, NC):
                az_copy(0, f).start()
            send_a(1, EARLY_A)

        @pl.when(t == COMBINE_A)
        def _():
            combine()

        return carry

    lax.fori_loop(1, 3, fill_step, 0)
    product(0)
    lax.fori_loop(3, NZ, fill_step, 0)
    lax.fori_loop(0, blocks + half * LAG + SWAP_LAG, step, 0)

    for i in range(total):
        gout[i * cap:(i + 1) * cap, :] = out4[i, 0:cap, :]
    grad_ref[...] = gout[...].astype(BF16)

    result = dense[...]
    for r in range(1, NY):
        d_copy(r).wait_recv()
        result += drecv[r - 1].astype(F32)
    mixed_ref[...] = result.astype(BF16)

    for d in range(1, NY):
        y_copy(d).wait_send()
        d_copy(d).wait_send()

    def sent_z(m, carry):
        for f in range(NC):
            if f == 0:
                @pl.when(m > 0)
                def _():
                    bz_copy(m, 0).wait_send()
                    az_copy(m, 0).wait_send()
            else:
                bz_copy(m, f).wait_send()
                az_copy(m, f).wait_send()
        @pl.when(m != 1)
        def _():
            for s in range(half):
                plus(m, s).wait_send()
                minus(m, s).wait_send()
            swap(m).wait_send()

        return carry

    lax.fori_loop(0, NZ, sent_z, 0)
    trade().wait_send()
    for s in range(half):
        traded_plus(s).wait_send()
        if s:
            traded_minus(s).wait_send()


def write(mixed_in, grad_in, mixed_out, grad_out):
    mixed_out[...] = mixed_in[...]
    grad_out[...] = grad_in[...]


def on_device(hidden_a, expert_weights, routes_a, gates_a, cotangent_b, routes_b, gates_b):
    total = NY * NZ * NC
    _, slots, ff = hidden_a.shape
    cap = slots // total
    tok, width = cotangent_b.shape
    wide = -(-width // 128) * 128
    half, msg, block = NX // 2, NY * cap, NY * cap * NC
    count = NZ * NC
    vm, dma = pltpu.VMEM, pltpu.SemaphoreType.DMA
    whole = pl.BlockSpec(memory_space=pltpu.VMEM)
    anywhere = pl.BlockSpec(memory_space=pl.ANY)
    mixed, grad = pl.pallas_call(
        functools.partial(body, cap),
        out_shape=(
            jax.ShapeDtypeStruct((tok, width), BF16),
            jax.ShapeDtypeStruct((slots, 128), BF16),
        ),
        in_specs=[anywhere] * 7,
        out_specs=(whole, whole),
        scratch_shapes=[
            vm(routes_a.T.shape, routes_a.dtype),
            vm(gates_a.T.shape, F32),
            vm((tok, width), BF16),
            vm(routes_b.T.shape, routes_b.dtype),
            vm(gates_b.T.shape, F32),
            vm((slots, ff), BF16),
            vm((width, ff), BF16),
            vm((NY, tok, wide), BF16),
            vm((2, 3, 8, NY * tok), F32),
            vm((total, 16, width), F32),
            vm((msg, width), F32),
            vm((count, msg, width), BF16),
            vm((count, msg, width), BF16),
            vm((count, msg, width), BF16),
            vm((count, msg, width), BF16),
            vm((2, slots, NY * tok), BF16),
            vm((NZ, NX, 2, block, 128), F32),
            vm((NZ, half, 2, block, 128), BF16),
            vm((NZ, half, 2, block, 128), BF16),
            vm((NZ, half, 2, block, 128), BF16),
            vm((NZ, half, 2, block, 128), BF16),
            vm((NZ, 2, block, 128), F32),
            vm((NZ, block, 128), BF16),
            vm((NZ, block, 128), BF16),
            vm((total, 16, 128), F32),
            vm((slots, 128), F32),
            vm((tok, width), F32),
            vm((NY - 1, tok, width), BF16),
            vm((NY - 1, tok, width), BF16),
            vm((2, block, 128), F32),
            vm((NX, block, 128), BF16),
            vm((NX, block, 128), BF16),
            dma((7,)),
            dma((NY - 1,)), dma((NY - 1,)),
            dma((count,)), dma((count,)),
            dma((count,)), dma((count,)),
            dma((NZ, half)), dma((NZ, half)),
            dma((NZ, half)), dma((NZ, half)),
            dma((NZ,)), dma((NZ,)),
            dma((NY - 1,)), dma((NY - 1,)), dma, dma,
        ],
        compiler_params=pltpu.CompilerParams(
            collective_id=0, has_side_effects=True,
            vmem_limit_bytes=56 * 1024 * 1024,
        ),
    )(
        hidden_a.reshape(slots, ff), expert_weights.reshape(ff, width).T,
        routes_a.T, gates_a.T, cotangent_b, routes_b.T, gates_b.T,
    )
    mixed, grad = pl.pallas_call(
        write,
        out_shape=(
            jax.ShapeDtypeStruct((tok, width), BF16),
            jax.ShapeDtypeStruct((slots, 128), BF16),
        ),
        in_specs=[whole, whole],
        out_specs=(whole, whole),
    )(mixed, grad)
    return mixed, grad.reshape(1, slots, 128)


def solution(mesh):
    in_specs = (
        P("expert", None, None),
        P("expert", None, "pipe"),
        P("expert", None),
        P("expert", None),
        P("expert", "pipe"),
        P("expert", None),
        P("expert", None),
    )
    out_specs = (P("expert", "pipe"), P("expert", None, "pipe"))
    return jax.shard_map(
        on_device, mesh=mesh, in_specs=in_specs, out_specs=out_specs, check_vma=False
    )
```
